256 devices in a mesh: fsdp: 32 (over z_lo, x, core), tp: 8 (over z_hi, y).
Axes of the slice: x: 4, y: 4, z: 8 (z_hi: 2, z_lo: 4; z = z_hi * 4 + z_lo), core: 2. Of those that a mesh axis runs over, the one named last changes fastest.
Arguments:
- activations: bfloat16 [16384, 4096], P(('fsdp', 'tp')), may hold values from -6 to 6
- weight: bfloat16 [4096, 7168], P('fsdp', 'tp'), may hold values from -0.09375 to 0.09375
- grad_out: bfloat16 [16384, 7168], P('fsdp', 'tp'), may hold values from -6 to 6
- sign_flips: int32 [128, 128], P('fsdp'), may hold values from -1 to 1, as said below
Outputs:
- forward_out: bfloat16 [16384, 7168], P('fsdp', 'tp')
- input_grad: bfloat16 [16384, 4096], P(('fsdp', 'tp'))
- weight_grad: bfloat16 [4096, 7168], P('fsdp', 'tp')
The draws below stay inside these ranges and needn't reach their ends.
Inputs may be any that keep to these rules, and one draw needn't show every extreme that they name: `sign_flips`: each entry is -1 or 1.
All inputs are finite; a program needn't handle non-finite values.
Results may differ from the reference program's by a relative error of at most 0.0057.
Values may be sent and summed in bfloat16 or wider, within the bound.
No kernel may reach another device: no remote copies, remote signals or barrier semaphores. Data moves between devices by JAX's collectives and lax.ppermute only.
A program may use at most 128 MiB of HBM per device.

```python
import jax
import jax.numpy as jnp
from jax import lax

D = 4096
HBLOCK = 128
QGROUP = 32
FF = 7168
TOKENS = 16384


def draw_sign_flips(key, part):
    key = jax.random.fold_in(key, 7)
    coin_flips = jax.random.randint(key, (TOKENS // HBLOCK, HBLOCK), 0, 2)
    return (2 * coin_flips - 1).astype(jnp.int32)


def block_scale(rng, shape, shards, smallest, high):
    loudness = 1.0
    for position, shards_of in shards:
        steps = jax.random.uniform(jax.random.fold_in(jax.random.fold_in(rng, 6), position), (shards_of,), jnp.float32, smallest / len(shards), high / len(shards))
        loudness = loudness * jnp.repeat(jnp.exp(steps), shape[position] // shards_of).reshape((-1,) + (1,) * (len(shape) - 1 - position))
    return loudness


def scatter_about(key, dims, spread, limit, pieces=(), held_as=jnp.bfloat16):
    factor_of = block_scale(key, dims, pieces, -0.22, 0.18) if pieces else 1.0
    result = jax.random.normal(key, dims, jnp.float32) * spread * factor_of
    return jnp.minimum(jnp.maximum(result, -limit), limit).astype(held_as)


def setup_inputs(seed: int = 0) -> dict:
    key_list = jax.random.split(jax.random.key(seed), 5)
    activations = scatter_about(key_list[0], (TOKENS, D), 1.0, 6.0, ((0, 256),))
    weight = scatter_about(key_list[1], (D, FF), D ** -0.5, 0.09375, ((0, 32), (1, 8)))
    grad_out = scatter_about(key_list[2], (TOKENS, FF), 1.0, 6.0, ((0, 32), (1, 8)))
    sign_flips = draw_sign_flips(jax.random.fold_in(key_list[4], 71), 0)
    return {"activations": activations, "weight": weight, "grad_out": grad_out, "sign_flips": sign_flips}


clip_factor = 1.5
sum_eps = 1e-06

def hadamard_table(length):
    index = jnp.arange(length, dtype=jnp.int32)
    parity = jnp.zeros((length, length), jnp.int32)
    for bit_number in range(length.bit_length() - 1):
        parity = parity + (index[:, None] >> bit_number & 1) * (index[None, :] >> bit_number & 1)
    return 1 - 2 * (parity % 2)

def rotate_clip(values, sign_flips):
    total_rows, columns = values.shape
    blocks = total_rows // HBLOCK
    hadamard = hadamard_table(HBLOCK).astype(jnp.float32)
    flipped = values.astype(jnp.float32).reshape(blocks, HBLOCK, columns) * sign_flips.astype(jnp.float32)[:, :, None]
    rotated = jnp.einsum('ij,bjc->bic', hadamard, flipped) * HBLOCK ** (-0.5)
    grouped = rotated.reshape(blocks, HBLOCK // QGROUP, QGROUP, columns)
    clip_bound = clip_factor * jnp.sqrt(lax.optimization_barrier(jnp.mean(grouped * grouped, axis=2, keepdims=True)) + sum_eps)
    return jnp.clip(grouped, -clip_bound, clip_bound).reshape(total_rows, columns).astype(jnp.bfloat16)

def reference(activations, weight, grad_out, sign_flips):
    forward_out = jnp.dot(activations, weight, preferred_element_type=jnp.float32).astype(jnp.bfloat16)
    input_grad = jnp.dot(grad_out, weight.T, preferred_element_type=jnp.float32).astype(jnp.bfloat16)
    x_quant = rotate_clip(activations, sign_flips)
    grad_quant = rotate_clip(grad_out, sign_flips)
    grad_scale = TOKENS ** (-0.5)
    weight_sum = jnp.dot(x_quant.T, grad_quant, preferred_element_type=jnp.float32) * grad_scale
    return (forward_out, input_grad, weight_sum.astype(jnp.bfloat16))
```

```python
import jax
import jax.numpy as jnp
from jax import lax
from jax.sharding import Mesh, PartitionSpec as P

HBLOCK = 128
QGROUP = 32
clip_factor = 1.5
sum_eps = 1e-06

Z, X, C, H, Y = 4, 4, 2, 2, 4
AXES = ("z", "x", "c", "h", "y")
SIZES = (Z, X, C, H, Y)


def flat(z, x, c, h, y):
    return (((z * X + x) * C + c) * H + h) * Y + y


def swap_pairs(**xor):
    d = [xor.get(a, 0) for a in AXES]
    pairs = []
    for z in range(Z):
        for x in range(X):
            for c in range(C):
                for h in range(H):
                    for y in range(Y):
                        t = [p ^ q for p, q in zip((z, x, c, h, y), d)]
                        pairs.append((flat(z, x, c, h, y), flat(*t)))
    return pairs


def swap(value, **xor):
    return lax.ppermute(value, AXES, swap_pairs(**xor))


def hadamard_table(length):
    index = jnp.arange(length, dtype=jnp.int32)
    parity = jnp.zeros((length, length), jnp.int32)
    for bit in range(length.bit_length() - 1):
        parity = parity + (index[:, None] >> bit & 1) * (index[None, :] >> bit & 1)
    return 1 - 2 * (parity % 2)


def rotate_clip(values, sign_flips):
    total_rows, columns = values.shape
    blocks = total_rows // HBLOCK
    hadamard = hadamard_table(HBLOCK).astype(jnp.bfloat16)
    flipped = values.reshape(blocks, HBLOCK, columns) * sign_flips.astype(jnp.bfloat16)[:, :, None]
    rotated = jnp.einsum(
        "ij,bjc->bic", hadamard, flipped, preferred_element_type=jnp.float32
    ) * HBLOCK ** (-0.5)
    grouped = rotated.reshape(blocks, HBLOCK // QGROUP, QGROUP, columns)
    clip_bound = clip_factor * jnp.sqrt(
        jnp.mean(grouped * grouped, axis=2, keepdims=True) + sum_eps
    )
    return (
        jnp.clip(grouped, -clip_bound, clip_bound).reshape(total_rows, columns).astype(jnp.bfloat16)
    )


def pick(pieces, index):
    return lax.dynamic_index_in_dim(jnp.stack(pieces), index, 0, keepdims=False)


def unxor(pieces, me):
    stacked = jnp.stack(pieces)
    return jnp.stack(
        [lax.dynamic_index_in_dim(stacked, me ^ k, 0, keepdims=False) for k in range(len(pieces))]
    )


def gather4(value, axis, split):
    a, b = split(value)
    a1 = swap(a, **{axis: 1})
    b1 = swap(b, **{axis: 3})
    a2 = swap(jnp.stack([a, a1]), **{axis: 3})
    b2 = swap(jnp.stack([b, b1]), **{axis: 1})
    return [a, a1, a2[1], a2[0]], [b, b2[0], b2[1], b1]


def per_device(activations, weight, grad_out, sign_flips):
    z, x, c, h, y = (lax.axis_index(a) for a in AXES)
    f32, bf16 = jnp.float32, jnp.bfloat16
    rows, d = activations.shape
    ff = weight.shape[1]
    tokens = rows * H * Y
    grad_scale = (tokens * Z * X * C) ** (-0.5)

    half = d // 2
    both = unxor([activations, swap(activations, h=1)], h)
    left, right = gather4(both, "y", lambda v: (v[..., :half], v[..., half:]))
    whole = jnp.concatenate([unxor(left, y), unxor(right, y)], axis=-1)
    whole_x = whole.transpose(1, 0, 2, 3).reshape(tokens, d)

    ws = [weight] + [swap(weight, z=k) for k in (1, 2, 3)]
    wz = unxor(ws, z)
    lo, hi = gather4(wz, "x", lambda v: (v[:2], v[2:]))
    wx = jnp.concatenate([unxor(lo, x), unxor(hi, x)], axis=1)
    wc = unxor([wx, swap(wx, c=1)], c)
    portion = wc.transpose(2, 1, 0, 3, 4).reshape(d, ff)

    forward_out = jnp.dot(whole_x, portion, preferred_element_type=f32).astype(bf16)

    ig = lax.dot_general(
        grad_out, portion, (((1,), (1,)), ((), ())), preferred_element_type=f32
    ).astype(bf16)
    ig = ig.reshape(H, Y, rows, d).transpose(1, 0, 2, 3)

    def scatter4(a, axis, me, first, second):
        rel = [lax.dynamic_index_in_dim(a, me ^ k, 0, keepdims=False) for k in range(4)]
        got = swap(jnp.stack([rel[first], rel[first ^ second]]), **{axis: first})
        mine = (rel[0].astype(f32) + got[0].astype(f32)).astype(bf16)
        other = (rel[second].astype(f32) + got[1].astype(f32)).astype(bf16)
        last = swap(other, **{axis: second})
        return mine.astype(f32) + last.astype(f32)

    left = scatter4(ig[..., :half], "y", y, 3, 1)
    right = scatter4(ig[..., half:], "y", y, 1, 3)
    ig = jnp.concatenate([left, right], axis=-1).astype(bf16)
    mine = lax.dynamic_index_in_dim(ig, h, 0, keepdims=False)
    other = lax.dynamic_index_in_dim(ig, 1 - h, 0, keepdims=False)
    input_grad = (mine.astype(f32) + swap(other, h=1).astype(f32)).astype(bf16)

    x_quant = rotate_clip(whole_x, sign_flips)
    grad_quant = rotate_clip(grad_out, sign_flips)
    wg = (
        lax.dot_general(x_quant, grad_quant, (((0,), (0,)), ((), ())), preferred_element_type=f32)
        * grad_scale
    ).astype(bf16)
    wg = wg.reshape(Z, X, C, d // (Z * X * C), ff).transpose(2, 1, 0, 3, 4)
    mine = lax.dynamic_index_in_dim(wg, c, 0, keepdims=False)
    other = lax.dynamic_index_in_dim(wg, 1 - c, 0, keepdims=False)
    wg = (mine.astype(f32) + swap(other, c=1).astype(f32)).astype(bf16)
    lo = scatter4(wg[:, :2], "x", x, 3, 1)
    hi = scatter4(wg[:, 2:], "x", x, 1, 3)
    wg = jnp.concatenate([lo, hi]).astype(bf16)
    total = lax.dynamic_index_in_dim(wg, z, 0, keepdims=False).astype(f32)
    for k in (1, 2, 3):
        total += swap(lax.dynamic_index_in_dim(wg, z ^ k, 0, keepdims=False), z=k).astype(f32)
    return forward_out, input_grad, total.astype(bf16)


def solution(mesh):
    fine = Mesh(mesh.devices.reshape(SIZES), AXES)
    fsdp, tp = ("z", "x", "c"), ("h", "y")
    return jax.shard_map(
        per_device,
        mesh=fine,
        in_specs=(P(fsdp + tp, None), P(fsdp, tp), P(fsdp, tp), P(fsdp, None)),
        out_specs=(P(fsdp, tp), P(fsdp + tp, None), P(fsdp, tp)),
        check_vma=False,
    )
```

```python
import functools

import jax
import jax.numpy as jnp
import numpy as np
from jax import lax
from jax.experimental import pallas as pl
from jax.experimental.pallas import tpu as pltpu
from jax.sharding import Mesh, PartitionSpec as P

HBLOCK = 128
QGROUP = 32
clip_factor = 1.5
sum_eps = 1e-06

Z, X, C, H, Y = 4, 4, 2, 2, 4
AXES = ("z", "x", "c", "h", "y")
SIZES = (Z, X, C, H, Y)
GROUPS = ((0,), (1,), (2,), (3,))

f32, bf16 = jnp.float32, jnp.bfloat16
VMEM = pl.BlockSpec(memory_space=pltpu.VMEM)
SMEM = pl.BlockSpec(memory_space=pltpu.SMEM)
PARAMS = pltpu.CompilerParams(vmem_limit_bytes=28 * 2**20)


def swap(value, axis, by):
    by = by if isinstance(by, tuple) else (by, by)
    k = AXES.index(axis)
    pairs = []
    for source in np.ndindex(*SIZES):
        target = list(source)
        target[k] ^= by[source[2]]
        pairs.append(
            tuple(int(np.ravel_multi_index(p, SIZES)) for p in (source, tuple(target)))
        )
    return lax.ppermute(value, AXES, pairs)


ONE_THREE, THREE_ONE = (1, 3), (3, 1)


def gather_slots(c):
    return (0, 1 + 2 * c, 3 - 2 * c, 2)


def scatter_slots(c):
    return (0, 1 + 2 * c, 3 - 2 * c, 2)


def gather4(value, axis):
    near = swap(value, axis, ONE_THREE)
    pair = jnp.stack([value, near])
    return pair, swap(pair, axis, THREE_ONE)


def scatter4(keep, send, axis):
    pair = keep.astype(f32) + swap(send, axis, THREE_ONE).astype(f32)
    return pair[0] + swap(pair[1].astype(bf16), axis, ONE_THREE).astype(f32)


def hadamard_table(length):
    index = np.arange(length)
    both = index[:, None] & index[None, :]
    parity = np.zeros((length, length), np.int64)
    for bit in range(length.bit_length() - 1):
        parity += both >> bit & 1
    return 1 - 2 * (parity % 2)


def rotate_clip(values, signed):
    rows, columns = values.shape
    rotated = jnp.dot(signed, values, preferred_element_type=f32) * HBLOCK ** (-0.5)
    grouped = rotated.reshape(rows // QGROUP, QGROUP, columns)
    bound = clip_factor * jnp.sqrt(
        jnp.mean(grouped * grouped, axis=1, keepdims=True) + sum_eps
    )
    return jnp.clip(grouped, -bound, bound).reshape(rows, columns).astype(bf16)


def signed_tables(table_ref, sign_ref):
    table = table_ref[...].astype(f32)
    signs = sign_ref[...].astype(f32)
    return [(table * signs[b : b + 1, :]).astype(bf16) for b in range(signs.shape[0])]


def prepare_kernel(pos, g_ref, sign_ref, table_ref, quant_ref, order_ref):
    c, h, y = pos[2], pos[3], pos[4]
    rows = order_ref.shape[2]
    columns = g_ref.shape[1]
    for slot, r in enumerate(scatter_slots(c)):
        for k in range(H):
            start = pl.multiple_of(((h ^ k) * Y + (y ^ r)) * rows, rows)
            order_ref[slot, k] = g_ref[pl.ds(start, rows), :]
    for b, signed in enumerate(signed_tables(table_ref, sign_ref)):
        block = pl.ds(b * HBLOCK, HBLOCK)
        for start in range(0, columns, 128):
            part = pl.ds(start, 128)
            quant_ref[block, part] = rotate_clip(g_ref[block, part], signed)


def weight_grad_kernel(
    scale, pos, near_ref, far_ref, sign_ref, table_ref, quant_ref, x_ref, keep_ref, later_ref, send_ref, rotated_ref
):
    x, c, h, y = pos[1], pos[2], pos[3], pos[4]
    rows = near_ref.shape[2]
    columns = near_ref.shape[3]
    n = columns // (X * C * 128)
    for slot, r in enumerate(gather_slots(c)):
        source = (near_ref, far_ref)[slot // 2]
        for k in range(H):
            start = pl.multiple_of(((h ^ k) * Y + (y ^ r)) * rows, rows)
            x_ref[pl.ds(start, rows), :] = source[slot % 2, k]
    tables = signed_tables(table_ref, sign_ref)
    place = 0
    for core in range(C):
        for r in scatter_slots(c ^ core):
            for i in range(n):
                start = ((i * X + (x ^ r)) * C + (c ^ core)) * 128
                part = pl.ds(pl.multiple_of(start, 128), 128)
                for b, signed in enumerate(tables):
                    block = pl.ds(b * HBLOCK, HBLOCK)
                    rotated_ref[block, pl.ds(place, 128)] = rotate_clip(x_ref[block, part], signed)
                place += 128
    quant = quant_ref[...]
    width = n * 256
    for step, (ref, at) in enumerate(((send_ref, 0), (send_ref, 2), (keep_ref, 0), (later_ref, 0))):
        step = (2, 3, 0, 1)[step]
        part = rotated_ref[:, step * width : (step + 1) * width]
        product = scale * lax.dot_general(
            part, quant, (((0,), (0,)), ((), ())), preferred_element_type=f32
        )
        ref[at : at + 2] = product.reshape(2, n, 128, -1).astype(ref.dtype)


def input_grad_kernel(pos, near_ref, far_ref, near2_ref, far2_ref, g_ref, w_ref, keep_ref, send_ref):
    x, c = pos[1], pos[2]
    n, _, _, depth, ff = w_ref.shape
    for core, (near, far) in enumerate(((near_ref, far_ref), (near2_ref, far2_ref))):
        for slot, r in enumerate(gather_slots(c ^ core)):
            for i in range(n):
                w_ref[i, x ^ r, c ^ core] = (near, far)[slot // 2][slot % 2, i]
    half = 2 * H * g_ref.shape[2]
    for i in range(n):
        w = w_ref[i].reshape(X * C * depth, ff)
        part = pl.ds(i * X * C * depth, X * C * depth)
        for k, ref in ((1, send_ref), (0, keep_ref)):
            g = g_ref[2 * k : 2 * k + 2].reshape(half, ff)
            product = lax.dot_general(g, w, (((1,), (1,)), ((), ())), preferred_element_type=f32)
            ref[:, :, :, part] = product.reshape(2, H, -1, X * C * depth).astype(ref.dtype)


def forward_kernel(*refs):
    out_ref = refs[-1]
    pairs = len(refs) // 2
    rows = out_ref.shape[0] // 2
    for half in range(2):
        part = pl.ds(half * rows, rows)
        total = None
        for x_ref, w_ref in zip(refs[:pairs], refs[pairs:-1]):
            term = jnp.dot(x_ref[part, :], w_ref[...], preferred_element_type=f32)
            total = term if total is None else total + term
        out_ref[part, :] = total.astype(out_ref.dtype)


def call(kernel, name, outs, args, flops, scratch=()):
    nbytes = sum(a.size * a.dtype.itemsize for a in (*args, *outs))
    return pl.pallas_call(
        kernel,
        out_shape=outs,
        in_specs=[SMEM if a.ndim == 1 else VMEM for a in args],
        out_specs=[VMEM] * len(outs),
        scratch_shapes=scratch,
        compiler_params=PARAMS,
        cost_estimate=pl.CostEstimate(flops=flops, bytes_accessed=nbytes, transcendentals=0),
        name=name,
    )(*args)


def per_device(activations, weight, grad_out, sign_flips):
    shape = jax.ShapeDtypeStruct
    z, x, c, h, y = (lax.axis_index(a) for a in AXES)
    pos = jnp.stack([z, x, c, h, y]).astype(jnp.int32)
    rows, d = activations.shape
    depth, ff = weight.shape
    tokens = rows * H * Y
    wide = d // Z
    scale = (tokens * Z * X * C) ** (-0.5)
    table = jnp.asarray(hadamard_table(HBLOCK), bf16)

    quant, order = call(
        prepare_kernel,
        "prepare",
        (shape((tokens, ff), bf16), shape((4, H, rows, ff), bf16)),
        (pos, grad_out, sign_flips, table),
        2 * tokens * HBLOCK * ff,
    )

    xs, ws, input_parts, weight_parts = [], [], {}, []
    for group in GROUPS:
        n = len(group)
        mine = jnp.concatenate(
            [lax.dynamic_slice(activations, (0, (z ^ r) * wide), (rows, wide)) for r in group], axis=1
        )
        both = jnp.stack([mine, swap(mine, "h", 1)])
        near, far = gather4(both, "y")
        w = jnp.stack([swap(weight, "z", r) if r else weight for r in group])
        w_near, w_far = gather4(w, "x")
        w_near2, w_far2 = swap(w_near, "c", 1), swap(w_far, "c", 1)

        whole, keep, send = call(
            input_grad_kernel,
            "input_grad",
            (
                shape((n, X, C, depth, ff), bf16),
                shape((2, H, rows, n * wide), f32),
                shape((2, H, rows, n * wide), bf16),
            ),
            (pos, w_near, w_far, w_near2, w_far2, order),
            2 * tokens * ff * n * wide,
        )
        ws.append(whole.reshape(n * wide, ff))
        pair = scatter4(keep, send, "y")
        part = pair[0] + swap(pair[1].astype(bf16), "h", 1).astype(f32)
        for i, r in enumerate(group):
            input_parts[r] = part[:, i * wide : (i + 1) * wide].astype(bf16)

        whole, keep, later, send = call(
            functools.partial(weight_grad_kernel, scale),
            "weight_grad",
            (
                shape((tokens, n * wide), bf16),
                shape((2, n, depth, ff), f32),
                shape((2, n, depth, ff), f32),
                shape((4, n, depth, ff), bf16),
            ),
            (pos, near, far, sign_flips, table, quant),
            2 * tokens * (ff + HBLOCK) * n * wide,
            [pltpu.VMEM((tokens, n * wide), bf16)],
        )
        xs.append(whole)
        got = swap(send, "c", 1).astype(f32)
        part = scatter4(keep + got[:2], (later + got[2:]).astype(bf16), "x")
        for i, r in enumerate(group):
            weight_parts.append(swap(part[i].astype(bf16), "z", r).astype(f32) if r else part[i])

    (forward_out,) = call(
        forward_kernel, "forward", (shape((tokens, ff), bf16),), (*xs, *ws), 2 * tokens * d * ff
    )
    stacked = jnp.stack([input_parts[r] for r in range(Z)])
    input_grad = jnp.concatenate(
        [lax.dynamic_index_in_dim(stacked, z ^ k, 0, keepdims=False) for k in range(Z)], axis=1
    )
    return forward_out, input_grad, sum(weight_parts).astype(bf16)


def solution(mesh):
    fine = Mesh(mesh.devices.reshape(SIZES), AXES)
    fsdp, tp = ("z", "x", "c"), ("h", "y")
    return jax.shard_map(
        per_device,
        mesh=fine,
        in_specs=(P(fsdp + tp, None), P(fsdp, tp), P(fsdp, tp), P(fsdp, None)),
        out_specs=(P(fsdp, tp), P(fsdp + tp, None), P(fsdp, tp)),
        check_vma=False,
    )
```

```python
import functools

import jax
import jax.numpy as jnp
import numpy as np
from jax import lax
from jax.experimental import pallas as pl
from jax.experimental.pallas import tpu as pltpu
from jax.sharding import Mesh, PartitionSpec as P

HBLOCK = 128
QGROUP = 32
clip_factor = 1.5
sum_eps = 1e-06

Z, X, C, H, Y = 4, 4, 2, 2, 4
AXES = ("z", "x", "c", "h", "y")
SIZES = (Z, X, C, H, Y)
FLOPS = 1000

f32, bf16 = jnp.float32, jnp.bfloat16
VMEM = pl.BlockSpec(memory_space=pltpu.VMEM)
SMEM = pl.BlockSpec(memory_space=pltpu.SMEM)
PARAMS = pltpu.CompilerParams(vmem_limit_bytes=20 * 2**20)


def swap(value, axis, by):
    by = by if isinstance(by, tuple) else (by, by)
    k = AXES.index(axis)
    pairs = []
    for source in np.ndindex(*SIZES):
        target = list(source)
        target[k] ^= by[source[2]]
        pairs.append(
            tuple(int(np.ravel_multi_index(p, SIZES)) for p in (source, tuple(target)))
        )
    return lax.ppermute(value, AXES, pairs)


ONE_THREE, THREE_ONE = (1, 3), (3, 1)


def gather_slots(c):
    return (0, 1 + 2 * c, 3 - 2 * c, 2)


def scatter_slots(c):
    return (0, 1 + 2 * c, 3 - 2 * c, 2)


def hadamard_table(length):
    index = np.arange(length)
    both = index[:, None] & index[None, :]
    parity = np.zeros((length, length), np.int64)
    for bit in range(length.bit_length() - 1):
        parity += both >> bit & 1
    return 1 - 2 * (parity % 2)


def rotate_clip(values, signed):
    rows, columns = values.shape
    rotated = jnp.dot(signed, values, preferred_element_type=f32) * HBLOCK ** (-0.5)
    grouped = rotated.reshape(rows // QGROUP, QGROUP, columns)
    bound = clip_factor * jnp.sqrt(
        jnp.mean(grouped * grouped, axis=1, keepdims=True) + sum_eps
    )
    return jnp.clip(grouped, -bound, bound).reshape(rows, columns).astype(bf16)


def signed_tables(table_ref, sign_ref):
    table = table_ref[...].astype(f32)
    signs = sign_ref[...].astype(f32)
    return [(table * signs[b : b + 1, :]).astype(bf16) for b in range(signs.shape[0])]


def prepare_kernel(pos, g_ref, sign_ref, table_ref, quant_ref, order_ref):
    c, h, y = pos[2], pos[3], pos[4]
    rows = order_ref.shape[2]
    columns = g_ref.shape[1]
    for slot, r in enumerate(scatter_slots(c)):
        for k in range(H):
            start = pl.multiple_of(((h ^ k) * Y + (y ^ r)) * rows, rows)
            order_ref[slot, k] = g_ref[pl.ds(start, rows), :]
    for b, signed in enumerate(signed_tables(table_ref, sign_ref)):
        block = pl.ds(b * HBLOCK, HBLOCK)
        for start in range(0, columns, 128):
            part = pl.ds(start, 128)
            quant_ref[block, part] = rotate_clip(g_ref[block, part], signed)


def weight_grad_kernel(
    scale, pos, near_ref, far_ref, sign_ref, table_ref, quant_ref, x_ref, keep_ref, later_ref, send_ref, rotated_ref
):
    x, c, h, y = pos[1], pos[2], pos[3], pos[4]
    rows = near_ref.shape[2]
    columns = near_ref.shape[3]
    n = columns // (X * C * 128)
    for slot, r in enumerate(gather_slots(c)):
        source = (near_ref, far_ref)[slot // 2]
        for k in range(H):
            start = pl.multiple_of(((h ^ k) * Y + (y ^ r)) * rows, rows)
            x_ref[pl.ds(start, rows), :] = source[slot % 2, k]
    tables = signed_tables(table_ref, sign_ref)
    place = 0
    for core in range(C):
        for r in scatter_slots(c ^ core):
            for i in range(n):
                start = ((i * X + (x ^ r)) * C + (c ^ core)) * 128
                part = pl.ds(pl.multiple_of(start, 128), 128)
                for b, signed in enumerate(tables):
                    block = pl.ds(b * HBLOCK, HBLOCK)
                    rotated_ref[block, pl.ds(place, 128)] = rotate_clip(x_ref[block, part], signed)
                place += 128
    quant = quant_ref[...]
    width = n * 256
    for step, (ref, at) in enumerate(((send_ref, 0), (send_ref, 2), (keep_ref, 0), (later_ref, 0))):
        step = (2, 3, 0, 1)[step]
        part = rotated_ref[:, step * width : (step + 1) * width]
        product = scale * lax.dot_general(
            part, quant, (((0,), (0,)), ((), ())), preferred_element_type=f32
        )
        ref[at : at + 2] = product.reshape(2, n, 128, -1).astype(ref.dtype)


def input_grad_kernel(pos, near_ref, far_ref, near2_ref, far2_ref, g_ref, w_ref, keep_ref, send_ref):
    x, c = pos[1], pos[2]
    n, _, _, depth, ff = w_ref.shape
    for core, (near, far) in enumerate(((near_ref, far_ref), (near2_ref, far2_ref))):
        for slot, r in enumerate(gather_slots(c ^ core)):
            for i in range(n):
                w_ref[i, x ^ r, c ^ core] = (near, far)[slot // 2][slot % 2, i]
    half = 2 * H * g_ref.shape[2]
    for i in range(n):
        w = w_ref[i].reshape(X * C * depth, ff)
        part = pl.ds(i * X * C * depth, X * C * depth)
        for k, ref in ((1, send_ref), (0, keep_ref)):
            g = g_ref[2 * k : 2 * k + 2].reshape(half, ff)
            product = lax.dot_general(g, w, (((1,), (1,)), ((), ())), preferred_element_type=f32)
            ref[:, :, :, part] = product.reshape(2, H, -1, X * C * depth).astype(ref.dtype)


def forward_kernel(*refs):
    out_ref = refs[-1]
    pairs = len(refs) // 2
    rows = out_ref.shape[0] // 2
    for half in range(2):
        part = pl.ds(half * rows, rows)
        total = None
        for x_ref, w_ref in zip(refs[:pairs], refs[pairs:-1]):
            term = jnp.dot(x_ref[part, :], w_ref[...], preferred_element_type=f32)
            total = term if total is None else total + term
        out_ref[part, :] = total.astype(out_ref.dtype)


def call(kernel, name, outs, args, flops, scratch=()):
    return pl.pallas_call(
        kernel,
        out_shape=outs,
        in_specs=[SMEM if a.ndim == 1 else VMEM for a in args],
        out_specs=[VMEM] * len(outs),
        scratch_shapes=scratch,
        compiler_params=PARAMS,
        cost_estimate=pl.CostEstimate(flops=flops, bytes_accessed=flops, transcendentals=0),
        name=name,
    )(*args)


def per_device(activations, weight, grad_out, sign_flips):
    shape = jax.ShapeDtypeStruct
    z, x, c, h, y = (lax.axis_index(a) for a in AXES)
    pos = jnp.stack([z, x, c, h, y]).astype(jnp.int32)
    rows, d = activations.shape
    depth, ff = weight.shape
    tokens = rows * H * Y
    wide = d // Z
    scale = (tokens * Z * X * C) ** (-0.5)
    table = jnp.asarray(hadamard_table(HBLOCK), bf16)

    quant, order = call(
        prepare_kernel,
        "prepare",
        (shape((tokens, ff), bf16), shape((4, H, rows, ff), bf16)),
        (pos, grad_out, sign_flips, table),
        FLOPS,
    )

    def slab(group):
        return jnp.concatenate(
            [lax.dynamic_slice(activations, (0, (z ^ r) * wide), (rows, wide)) for r in group], axis=1
        )

    def input_grad_terms(group, near, far, near2, far2):
        n = len(group)
        whole, keep, send = call(
            input_grad_kernel,
            "input_grad",
            (
                shape((n, X, C, depth, ff), bf16),
                shape((2, H, rows, n * wide), f32),
                shape((2, H, rows, n * wide), bf16),
            ),
            (pos, near, far, near2, far2, order),
            FLOPS,
        )
        return whole.reshape(n * wide, ff), keep, send

    def weight_grad_terms(group, near, far):
        n = len(group)
        return call(
            functools.partial(weight_grad_kernel, scale),
            "weight_grad",
            (
                shape((tokens, n * wide), bf16),
                shape((2, n, depth, ff), f32),
                shape((2, n, depth, ff), f32),
                shape((4, n, depth, ff), bf16),
            ),
            (pos, near, far, sign_flips, table, quant),
            FLOPS,
            [pltpu.VMEM((tokens, n * wide), bf16)],
        )

    def step1(keep, send, axis):
        pair = keep.astype(f32) + swap(send, axis, THREE_ONE).astype(f32)
        return pair[0], pair[1].astype(bf16)

    def step2(keep, send, axis):
        return keep + swap(send, axis, ONE_THREE).astype(f32)

    def core_sum(keep, later, send):
        got = swap(send, "c", 1).astype(f32)
        return keep + got[:2], (later + got[2:]).astype(bf16)

    bar = lambda *values: lax.optimization_barrier(values)

    (x2, x3), (w0, w1) = (2, 3), (0, 1)
    xa_own, xb_own = slab((x2, x3)), slab((w0, w1))
    wa = jnp.stack([weight, swap(weight, "z", 1)])
    xa = jnp.stack([xa_own, swap(xa_own, "h", 1)])
    wa_near = jnp.stack([wa, swap(wa, "x", ONE_THREE)])
    xa, wa_near, xb_own, quant, order, weight = bar(xa, wa_near, xb_own, quant, order, weight)
    xb = jnp.stack([xb_own, swap(xb_own, "h", 1)])
    wa_far = swap(wa_near, "x", THREE_ONE)
    xa_near = jnp.stack([xa, swap(xa, "y", ONE_THREE)])
    xb, wa_near, wa_far, xa_near, weight = bar(xb, wa_near, wa_far, xa_near, weight)
    w2 = swap(weight, "z", 2)
    xa_far = swap(xa_near, "y", THREE_ONE)
    wa_whole, ia_keep, ia_send = input_grad_terms(
        (w0, w1), wa_near, wa_far, swap(wa_near, "c", 1), swap(wa_far, "c", 1)
    )
    w2, xa_near, xa_far, ia_keep, ia_send, weight = bar(w2, xa_near, xa_far, ia_keep, ia_send, weight)
    w3 = swap(weight, "z", 3)
    ia_keep, ia_send = step1(ia_keep, ia_send, "y")
    xa_whole, ga_keep, ga_later, ga_send = weight_grad_terms((x2, x3), xa_near, xa_far)
    ga_keep, ga_send = core_sum(ga_keep, ga_later, ga_send)
    wb = jnp.stack([w2, w3])
    wb, ia_keep, ia_send, ga_keep, ga_send, xb = bar(wb, ia_keep, ia_send, ga_keep, ga_send, xb)
    xb_near = jnp.stack([xb, swap(xb, "y", ONE_THREE)])
    ia = step2(ia_keep, ia_send, "y")
    ia_send = ia[1].astype(bf16)
    ga_keep, ga_send = step1(ga_keep, ga_send, "x")
    xb_near, ia, ia_send, ga_keep, ga_send, wb = bar(xb_near, ia, ia_send, ga_keep, ga_send, wb)
    ia = (ia[0] + swap(ia_send, "h", 1).astype(f32)).astype(bf16)
    xb_far = swap(xb_near, "y", THREE_ONE)
    wb_near = jnp.stack([wb, swap(wb, "x", ONE_THREE)])
    ga = step2(ga_keep, ga_send, "x").astype(bf16)
    ia, xb_near, xb_far, wb_near, ga = bar(ia, xb_near, xb_far, wb_near, ga)
    g2 = swap(ga[0], "z", 2)
    wb_far = swap(wb_near, "x", THREE_ONE)
    xb_whole, gb_keep, gb_later, gb_send = weight_grad_terms((w0, w1), xb_near, xb_far)
    gb_keep, gb_send = core_sum(gb_keep, gb_later, gb_send)
    g2, wb_near, wb_far, gb_keep, gb_send, ga = bar(g2, wb_near, wb_far, gb_keep, gb_send, ga)
    g3 = swap(ga[1], "z", 3)
    gb_keep, gb_send = step1(gb_keep, gb_send, "x")
    wb_whole, ib_keep, ib_send = input_grad_terms(
        (x2, x3), wb_near, wb_far, swap(wb_near, "c", 1), swap(wb_far, "c", 1)
    )
    ib_keep, ib_send = step1(ib_keep, ib_send, "y")
    gb = step2(gb_keep, gb_send, "x")
    g1 = swap(gb[1].astype(bf16), "z", 1)
    ib = step2(ib_keep, ib_send, "y")
    ib_send = ib[1].astype(bf16)
    ib, ib_send, xa_whole, xb_whole, wa_whole, wb_whole = bar(
        ib, ib_send, xa_whole, xb_whole, wa_whole, wb_whole
    )
    ib = (ib[0] + swap(ib_send, "h", 1).astype(f32)).astype(bf16)
    (forward_out,) = call(
        forward_kernel,
        "forward",
        (shape((tokens, ff), bf16),),
        (xa_whole, xb_whole, wb_whole, wa_whole),
        FLOPS,
    )
    weight_grad = (gb[0] + g1.astype(f32) + g2.astype(f32) + g3.astype(f32)).astype(bf16)
    parts = [ia[:, :wide], ia[:, wide:], ib[:, :wide], ib[:, wide:]]
    stacked = jnp.stack(parts)
    input_grad = jnp.concatenate(
        [lax.dynamic_index_in_dim(stacked, z ^ k, 0, keepdims=False) for k in range(Z)], axis=1
    )
    return forward_out, input_grad, weight_grad


def solution(mesh):
    fine = Mesh(mesh.devices.reshape(SIZES), AXES)
    fsdp, tp = ("z", "x", "c"), ("h", "y")
    return jax.shard_map(
        per_device,
        mesh=fine,
        in_specs=(P(fsdp + tp, None), P(fsdp, tp), P(fsdp, tp), P(fsdp, None)),
        out_specs=(P(fsdp, tp), P(fsdp + tp, None), P(fsdp, tp)),
        check_vma=False,
    )
```

```python
import functools

import jax
import jax.numpy as jnp
import numpy as np
from jax import lax
from jax.experimental import pallas as pl
from jax.experimental.pallas import tpu as pltpu
from jax.sharding import Mesh, PartitionSpec as P

HBLOCK = 128
QGROUP = 32
clip_factor = 1.5
sum_eps = 1e-06

Z, X, C, H, Y = 4, 4, 2, 2, 4
AXES = ("z", "x", "c", "h", "y")
SIZES = (Z, X, C, H, Y)
FLOPS = 1000

f32, bf16 = jnp.float32, jnp.bfloat16
VMEM = pl.BlockSpec(memory_space=pltpu.VMEM)
SMEM = pl.BlockSpec(memory_space=pltpu.SMEM)
PARAMS = pltpu.CompilerParams(vmem_limit_bytes=20 * 2**20)


def swap(value, axis, by):
    by = by if isinstance(by, tuple) else (by, by)
    k = AXES.index(axis)
    pairs = []
    for source in np.ndindex(*SIZES):
        target = list(source)
        target[k] ^= by[source[2]]
        pairs.append(
            tuple(int(np.ravel_multi_index(p, SIZES)) for p in (source, tuple(target)))
        )
    return lax.ppermute(value, AXES, pairs)


ONE_THREE, THREE_ONE = (1, 3), (3, 1)


def gather_slots(c):
    return (0, 1 + 2 * c, 3 - 2 * c, 2)


def scatter_slots(c):
    return (0, 1 + 2 * c, 3 - 2 * c, 2)


def hadamard_table(length):
    index = np.arange(length)
    both = index[:, None] & index[None, :]
    parity = np.zeros((length, length), np.int64)
    for bit in range(length.bit_length() - 1):
        parity += both >> bit & 1
    return 1 - 2 * (parity % 2)


def rotate_clip(values, signed):
    rows, columns = values.shape
    rotated = jnp.dot(signed, values, preferred_element_type=f32) * HBLOCK ** (-0.5)
    grouped = rotated.reshape(rows // QGROUP, QGROUP, columns)
    bound = clip_factor * jnp.sqrt(
        jnp.mean(grouped * grouped, axis=1, keepdims=True) + sum_eps
    )
    return jnp.clip(grouped, -bound, bound).reshape(rows, columns).astype(bf16)


def signed_tables(table_ref, sign_ref):
    table = table_ref[...].astype(f32)
    signs = sign_ref[...].astype(f32)
    return [(table * signs[b : b + 1, :]).astype(bf16) for b in range(signs.shape[0])]


def prepare_kernel(pos, g_ref, sign_ref, table_ref, quant_ref, order_ref):
    c, h, y = pos[2], pos[3], pos[4]
    rows = order_ref.shape[2]
    columns = g_ref.shape[1]
    for slot, r in enumerate(scatter_slots(c)):
        for k in range(H):
            start = pl.multiple_of(((h ^ k) * Y + (y ^ r)) * rows, rows)
            order_ref[slot, k] = g_ref[pl.ds(start, rows), :]
    for b, signed in enumerate(signed_tables(table_ref, sign_ref)):
        block = pl.ds(b * HBLOCK, HBLOCK)
        for start in range(0, columns, 128):
            part = pl.ds(start, 128)
            quant_ref[block, part] = rotate_clip(g_ref[block, part], signed)


def weight_grad_kernel(
    scale, pos, near_ref, far_ref, sign_ref, table_ref, quant_ref, x_ref, keep_ref, later_ref, send_ref, rotated_ref
):
    x, c, h, y = pos[1], pos[2], pos[3], pos[4]
    rows = near_ref.shape[2]
    columns = near_ref.shape[3]
    n = columns // (X * C * 128)
    for slot, r in enumerate(gather_slots(c)):
        source = (near_ref, far_ref)[slot // 2]
        for k in range(H):
            start = pl.multiple_of(((h ^ k) * Y + (y ^ r)) * rows, rows)
            x_ref[pl.ds(start, rows), :] = source[slot % 2, k]
    tables = signed_tables(table_ref, sign_ref)
    place = 0
    for core in range(C):
        for r in scatter_slots(c ^ core):
            for i in range(n):
                start = ((i * X + (x ^ r)) * C + (c ^ core)) * 128
                part = pl.ds(pl.multiple_of(start, 128), 128)
                for b, signed in enumerate(tables):
                    block = pl.ds(b * HBLOCK, HBLOCK)
                    rotated_ref[block, pl.ds(place, 128)] = rotate_clip(x_ref[block, part], signed)
                place += 128
    quant = quant_ref[...]
    width = n * 256
    for step, (ref, at) in enumerate(((send_ref, 0), (send_ref, 2), (keep_ref, 0), (later_ref, 0))):
        step = (2, 3, 0, 1)[step]
        part = rotated_ref[:, step * width : (step + 1) * width]
        product = scale * lax.dot_general(
            part, quant, (((0,), (0,)), ((), ())), preferred_element_type=f32
        )
        ref[at : at + 2] = product.reshape(2, n, 128, -1).astype(ref.dtype)


def input_grad_kernel(pos, near_ref, far_ref, near2_ref, far2_ref, g_ref, w_ref, keep_ref, send_ref):
    x, c = pos[1], pos[2]
    n, _, _, depth, ff = w_ref.shape
    for core, (near, far) in enumerate(((near_ref, far_ref), (near2_ref, far2_ref))):
        for slot, r in enumerate(gather_slots(c ^ core)):
            for i in range(n):
                w_ref[i, x ^ r, c ^ core] = (near, far)[slot // 2][slot % 2, i]
    half = 2 * H * g_ref.shape[2]
    for i in range(n):
        w = w_ref[i].reshape(X * C * depth, ff)
        part = pl.ds(i * X * C * depth, X * C * depth)
        for k, ref in ((1, send_ref), (0, keep_ref)):
            g = g_ref[2 * k : 2 * k + 2].reshape(half, ff)
            product = lax.dot_general(g, w, (((1,), (1,)), ((), ())), preferred_element_type=f32)
            ref[:, :, :, part] = product.reshape(2, H, -1, X * C * depth).astype(ref.dtype)


def forward_kernel(*refs):
    out_ref = refs[-1]
    pairs = len(refs) // 2
    rows = out_ref.shape[0] // 2
    for half in range(2):
        part = pl.ds(half * rows, rows)
        total = None
        for x_ref, w_ref in zip(refs[:pairs], refs[pairs:-1]):
            term = jnp.dot(x_ref[part, :], w_ref[...], preferred_element_type=f32)
            total = term if total is None else total + term
        out_ref[part, :] = total.astype(out_ref.dtype)


def call(kernel, name, outs, args, flops, scratch=()):
    return pl.pallas_call(
        kernel,
        out_shape=outs,
        in_specs=[SMEM if a.ndim == 1 else VMEM for a in args],
        out_specs=[VMEM] * len(outs),
        scratch_shapes=scratch,
        compiler_params=PARAMS,
        cost_estimate=pl.CostEstimate(flops=flops, bytes_accessed=flops, transcendentals=0),
        name=name,
    )(*args)


def per_device(activations, weight, grad_out, sign_flips):
    shape = jax.ShapeDtypeStruct
    z, x, c, h, y = (lax.axis_index(a) for a in AXES)
    pos = jnp.stack([z, x, c, h, y]).astype(jnp.int32)
    rows, d = activations.shape
    depth, ff = weight.shape
    tokens = rows * H * Y
    wide = d // Z
    scale = (tokens * Z * X * C) ** (-0.5)
    table = jnp.asarray(hadamard_table(HBLOCK), bf16)

    quant, order = call(
        prepare_kernel,
        "prepare",
        (shape((tokens, ff), bf16), shape((4, H, rows, ff), bf16)),
        (pos, grad_out, sign_flips, table),
        FLOPS,
    )

    def slab(group):
        return jnp.concatenate(
            [lax.dynamic_slice(activations, (0, (z ^ r) * wide), (rows, wide)) for r in group], axis=1
        )

    def input_grad_terms(group, near, far, near2, far2):
        n = len(group)
        whole, keep, send = call(
            input_grad_kernel,
            "input_grad",
            (
                shape((n, X, C, depth, ff), bf16),
                shape((2, H, rows, n * wide), f32),
                shape((2, H, rows, n * wide), bf16),
            ),
            (pos, near, far, near2, far2, order),
            FLOPS,
        )
        return whole.reshape(n * wide, ff), keep, send

    def weight_grad_terms(group, near, far):
        n = len(group)
        return call(
            functools.partial(weight_grad_kernel, scale),
            "weight_grad",
            (
                shape((tokens, n * wide), bf16),
                shape((2, n, depth, ff), f32),
                shape((2, n, depth, ff), f32),
                shape((4, n, depth, ff), bf16),
            ),
            (pos, near, far, sign_flips, table, quant),
            FLOPS,
            [pltpu.VMEM((tokens, n * wide), bf16)],
        )

    def step1(keep, send, axis):
        pair = keep.astype(f32) + swap(send, axis, THREE_ONE).astype(f32)
        return pair[0], pair[1].astype(bf16)

    def step2(keep, send, axis):
        return keep + swap(send, axis, ONE_THREE).astype(f32)

    def core_sum(keep, later, send):
        got = swap(send, "c", 1).astype(f32)
        return keep + got[:2], (later + got[2:]).astype(bf16)

    bar = lambda *values: lax.optimization_barrier(values)

    (x2, x3), (w0, w1) = (2, 3), (0, 1)
    xa_own, xb_own = slab((x2, x3)), slab((w0, w1))
    wa = jnp.stack([weight, swap(weight, "z", 1)])
    xa = jnp.stack([xa_own, swap(xa_own, "h", 1)])
    wa_near = jnp.stack([wa, swap(wa, "x", ONE_THREE)])
    xa, wa_near, xb_own, quant, order, weight = bar(xa, wa_near, xb_own, quant, order, weight)
    xb = jnp.stack([xb_own, swap(xb_own, "h", 1)])
    wa_far = swap(wa_near, "x", THREE_ONE)
    xa_near = jnp.stack([xa, swap(xa, "y", ONE_THREE)])
    xb, wa_near, wa_far, xa_near, weight = bar(xb, wa_near, wa_far, xa_near, weight)
    w2 = swap(weight, "z", 2)
    xa_far = swap(xa_near, "y", THREE_ONE)
    wa_whole, ia_keep, ia_send = input_grad_terms(
        (w0, w1), wa_near, wa_far, swap(wa_near, "c", 1), swap(wa_far, "c", 1)
    )
    w2, xa_near, xa_far, ia_keep, ia_send, weight = bar(w2, xa_near, xa_far, ia_keep, ia_send, weight)
    w3 = swap(weight, "z", 3)
    ia_keep, ia_send = step1(ia_keep, ia_send, "y")
    xa_whole, ga_keep, ga_later, ga_send = weight_grad_terms((x2, x3), xa_near, xa_far)
    ga_keep, ga_send = core_sum(ga_keep, ga_later, ga_send)
    wb = jnp.stack([w2, w3])
    wb, ia_keep, ia_send, ga_keep, ga_send, xb = bar(wb, ia_keep, ia_send, ga_keep, ga_send, xb)
    xb_near = jnp.stack([xb, swap(xb, "y", ONE_THREE)])
    ia = step2(ia_keep, ia_send, "y")
    ia_send = ia[1].astype(bf16)
    ga_keep, ga_send = step1(ga_keep, ga_send, "x")
    wb_near = jnp.stack([wb, swap(wb, "x", ONE_THREE)])
    xb_near, ia, ia_send, ga_keep, ga_send, wb_near = bar(xb_near, ia, ia_send, ga_keep, ga_send, wb_near)
    ia = (ia[0] + swap(ia_send, "h", 1).astype(f32)).astype(bf16)
    xb_far = swap(xb_near, "y", THREE_ONE)
    wb_far = swap(wb_near, "x", THREE_ONE)
    ia, xb_near, xb_far, wb_near, wb_far, ga_keep, ga_send = bar(
        ia, xb_near, xb_far, wb_near, wb_far, ga_keep, ga_send
    )
    ga = step2(ga_keep, ga_send, "x").astype(bf16)
    wb_near2, wb_far2 = swap(wb_near, "c", 1), swap(wb_far, "c", 1)
    xb_whole, gb_keep, gb_later, gb_send = weight_grad_terms((w0, w1), xb_near, xb_far)
    wb_near, wb_far, wb_near2, wb_far2, gb_send, ga = bar(wb_near, wb_far, wb_near2, wb_far2, gb_send, ga)
    gb_keep, gb_send = core_sum(gb_keep, gb_later, gb_send)
    wb_whole, ib_keep, ib_send = input_grad_terms((x2, x3), wb_near, wb_far, wb_near2, wb_far2)
    gb_keep, gb_send, ib_keep, ib_send, ga = bar(gb_keep, gb_send, ib_keep, ib_send, ga)
    g2 = swap(ga[0], "z", 2)
    ib_keep, ib_send = step1(ib_keep, ib_send, "y")
    gb_keep, gb_send = step1(gb_keep, gb_send, "x")
    g2, ib_keep, ib_send, gb_keep, gb_send, ga = bar(g2, ib_keep, ib_send, gb_keep, gb_send, ga)
    g3 = swap(ga[1], "z", 3)
    ib = step2(ib_keep, ib_send, "y")
    gb = step2(gb_keep, gb_send, "x")
    ib_send, g1 = ib[1].astype(bf16), gb[1].astype(bf16)
    ib, ib_send, gb, g1, g3, xa_whole, xb_whole, wa_whole, wb_whole = bar(
        ib, ib_send, gb, g1, g3, xa_whole, xb_whole, wa_whole, wb_whole
    )
    g1 = swap(g1, "z", 1)
    ib = (ib[0] + swap(ib_send, "h", 1).astype(f32)).astype(bf16)
    (forward_out,) = call(
        forward_kernel,
        "forward",
        (shape((tokens, ff), bf16),),
        (xa_whole, xb_whole, wb_whole, wa_whole),
        FLOPS,
    )
    weight_grad = (gb[0] + g1.astype(f32) + g2.astype(f32) + g3.astype(f32)).astype(bf16)
    parts = [ia[:, :wide], ia[:, wide:], ib[:, :wide], ib[:, wide:]]
    stacked = jnp.stack(parts)
    input_grad = jnp.concatenate(
        [lax.dynamic_index_in_dim(stacked, z ^ k, 0, keepdims=False) for k in range(Z)], axis=1
    )
    return forward_out, input_grad, weight_grad


def solution(mesh):
    fine = Mesh(mesh.devices.reshape(SIZES), AXES)
    fsdp, tp = ("z", "x", "c"), ("h", "y")
    return jax.shard_map(
        per_device,
        mesh=fine,
        in_specs=(P(fsdp + tp, None), P(fsdp, tp), P(fsdp, tp), P(fsdp, None)),
        out_specs=(P(fsdp, tp), P(fsdp + tp, None), P(fsdp, tp)),
        check_vma=False,
    )
```

```python
import functools

import jax
import jax.numpy as jnp
import numpy as np
from jax import lax
from jax.experimental import pallas as pl
from jax.experimental.pallas import tpu as pltpu
from jax.sharding import Mesh, PartitionSpec as P

HBLOCK = 128
QGROUP = 32
clip_factor = 1.5
sum_eps = 1e-06

Z, X, C, H, Y = 4, 4, 2, 2, 4
AXES = ("z", "x", "c", "h", "y")
SIZES = (Z, X, C, H, Y)
FLOPS = 1000

f32, bf16 = jnp.float32, jnp.bfloat16
VMEM = pl.BlockSpec(memory_space=pltpu.VMEM)
SMEM = pl.BlockSpec(memory_space=pltpu.SMEM)
PARAMS = pltpu.CompilerParams(vmem_limit_bytes=20 * 2**20)


def swap(value, axis, by):
    by = by if isinstance(by, tuple) else (by, by)
    k = AXES.index(axis)
    pairs = []
    for source in np.ndindex(*SIZES):
        target = list(source)
        target[k] ^= by[source[2]]
        pairs.append(
            tuple(int(np.ravel_multi_index(p, SIZES)) for p in (source, tuple(target)))
        )
    return lax.ppermute(value, AXES, pairs)


ONE_THREE, THREE_ONE = (1, 3), (3, 1)


def gather_slots(c):
    return (0, 1 + 2 * c, 3 - 2 * c, 2)


def scatter_slots(c):
    return (0, 1 + 2 * c, 3 - 2 * c, 2)


def hadamard_table(length):
    index = np.arange(length)
    both = index[:, None] & index[None, :]
    parity = np.zeros((length, length), np.int64)
    for bit in range(length.bit_length() - 1):
        parity += both >> bit & 1
    return 1 - 2 * (parity % 2)


def rotate_clip(values, signed):
    rows, columns = values.shape
    rotated = jnp.dot(signed, values, preferred_element_type=f32) * HBLOCK ** (-0.5)
    grouped = rotated.reshape(rows // QGROUP, QGROUP, columns)
    bound = clip_factor * jnp.sqrt(
        jnp.mean(grouped * grouped, axis=1, keepdims=True) + sum_eps
    )
    return jnp.clip(grouped, -bound, bound).reshape(rows, columns).astype(bf16)


def signed_tables(table_ref, sign_ref):
    table = table_ref[...].astype(f32)
    signs = sign_ref[...].astype(f32)
    return [(table * signs[b : b + 1, :]).astype(bf16) for b in range(signs.shape[0])]


def prepare_kernel(pos, g_ref, sign_ref, table_ref, quant_ref, order_ref):
    c, h, y = pos[2], pos[3], pos[4]
    rows = order_ref.shape[2]
    columns = g_ref.shape[1]
    for slot, r in enumerate(scatter_slots(c)):
        for k in range(H):
            start = pl.multiple_of(((h ^ k) * Y + (y ^ r)) * rows, rows)
            order_ref[slot, k] = g_ref[pl.ds(start, rows), :]
    for b, signed in enumerate(signed_tables(table_ref, sign_ref)):
        block = pl.ds(b * HBLOCK, HBLOCK)
        for start in range(0, columns, 128):
            part = pl.ds(start, 128)
            quant_ref[block, part] = rotate_clip(g_ref[block, part], signed)


def weight_grad_kernel(
    scale, pos, near_ref, far_ref, sign_ref, table_ref, quant_ref, x_ref, keep_ref, later_ref, send_ref, rotated_ref
):
    x, c, h, y = pos[1], pos[2], pos[3], pos[4]
    rows = near_ref.shape[2]
    columns = near_ref.shape[3]
    n = columns // (X * C * 128)
    for slot, r in enumerate(gather_slots(c)):
        source = (near_ref, far_ref)[slot // 2]
        for k in range(H):
            start = pl.multiple_of(((h ^ k) * Y + (y ^ r)) * rows, rows)
            x_ref[pl.ds(start, rows), :] = source[slot % 2, k]
    tables = signed_tables(table_ref, sign_ref)
    place = 0
    for core in range(C):
        for r in scatter_slots(c ^ core):
            for i in range(n):
                start = ((i * X + (x ^ r)) * C + (c ^ core)) * 128
                part = pl.ds(pl.multiple_of(start, 128), 128)
                for b, signed in enumerate(tables):
                    block = pl.ds(b * HBLOCK, HBLOCK)
                    rotated_ref[block, pl.ds(place, 128)] = rotate_clip(x_ref[block, part], signed)
                place += 128
    quant = quant_ref[...]
    width = n * 256
    for step, (ref, at) in enumerate(((send_ref, 0), (send_ref, 2), (keep_ref, 0), (later_ref, 0))):
        step = (2, 3, 0, 1)[step]
        part = rotated_ref[:, step * width : (step + 1) * width]
        product = scale * lax.dot_general(
            part, quant, (((0,), (0,)), ((), ())), preferred_element_type=f32
        )
        ref[at : at + 2] = product.reshape(2, n, 128, -1).astype(ref.dtype)


def input_grad_kernel(pos, near_ref, far_ref, near2_ref, far2_ref, g_ref, w_ref, keep_ref, send_ref):
    x, c = pos[1], pos[2]
    n, _, _, depth, ff = w_ref.shape
    for core, (near, far) in enumerate(((near_ref, far_ref), (near2_ref, far2_ref))):
        for slot, r in enumerate(gather_slots(c ^ core)):
            for i in range(n):
                w_ref[i, x ^ r, c ^ core] = (near, far)[slot // 2][slot % 2, i]
    half = 2 * H * g_ref.shape[2]
    for i in range(n):
        w = w_ref[i].reshape(X * C * depth, ff)
        part = pl.ds(i * X * C * depth, X * C * depth)
        for k, ref in ((1, send_ref), (0, keep_ref)):
            g = g_ref[2 * k : 2 * k + 2].reshape(half, ff)
            product = lax.dot_general(g, w, (((1,), (1,)), ((), ())), preferred_element_type=f32)
            ref[:, :, :, part] = product.reshape(2, H, -1, X * C * depth).astype(ref.dtype)


def forward_kernel(*refs):
    out_ref = refs[-1]
    pairs = len(refs) // 2
    rows = out_ref.shape[0] // 2
    for half in range(2):
        part = pl.ds(half * rows, rows)
        total = None
        for x_ref, w_ref in zip(refs[:pairs], refs[pairs:-1]):
            term = jnp.dot(x_ref[part, :], w_ref[...], preferred_element_type=f32)
            total = term if total is None else total + term
        out_ref[part, :] = total.astype(out_ref.dtype)


def call(kernel, name, outs, args, flops, scratch=()):
    return pl.pallas_call(
        kernel,
        out_shape=outs,
        in_specs=[SMEM if a.ndim == 1 else VMEM for a in args],
        out_specs=[VMEM] * len(outs),
        scratch_shapes=scratch,
        compiler_params=PARAMS,
        cost_estimate=pl.CostEstimate(flops=flops, bytes_accessed=flops, transcendentals=0),
        name=name,
    )(*args)


def per_device(activations, weight, grad_out, sign_flips):
    shape = jax.ShapeDtypeStruct
    z, x, c, h, y = (lax.axis_index(a) for a in AXES)
    pos = jnp.stack([z, x, c, h, y]).astype(jnp.int32)
    rows, d = activations.shape
    depth, ff = weight.shape
    tokens = rows * H * Y
    wide = d // Z
    scale = (tokens * Z * X * C) ** (-0.5)
    table = jnp.asarray(hadamard_table(HBLOCK), bf16)

    quant, order = call(
        prepare_kernel,
        "prepare",
        (shape((tokens, ff), bf16), shape((4, H, rows, ff), bf16)),
        (pos, grad_out, sign_flips, table),
        FLOPS,
    )

    def slab(group):
        return jnp.concatenate(
            [lax.dynamic_slice(activations, (0, (z ^ r) * wide), (rows, wide)) for r in group], axis=1
        )

    def input_grad_terms(group, near, far, near2, far2):
        n = len(group)
        whole, keep, send = call(
            input_grad_kernel,
            "input_grad",
            (
                shape((n, X, C, depth, ff), bf16),
                shape((2, H, rows, n * wide), f32),
                shape((2, H, rows, n * wide), bf16),
            ),
            (pos, near, far, near2, far2, order),
            FLOPS,
        )
        return whole.reshape(n * wide, ff), keep, send

    def weight_grad_terms(group, near, far):
        n = len(group)
        return call(
            functools.partial(weight_grad_kernel, scale),
            "weight_grad",
            (
                shape((tokens, n * wide), bf16),
                shape((2, n, depth, ff), f32),
                shape((2, n, depth, ff), f32),
                shape((4, n, depth, ff), bf16),
            ),
            (pos, near, far, sign_flips, table, quant),
            FLOPS,
            [pltpu.VMEM((tokens, n * wide), bf16)],
        )

    def step1(keep, send, axis):
        pair = keep.astype(f32) + swap(send, axis, THREE_ONE).astype(f32)
        return pair, pair[1].astype(bf16)

    def step2(keep, send, axis):
        return keep[0] + swap(send, axis, ONE_THREE).astype(f32)

    def core_sum(keep, later, send):
        got = swap(send, "c", 1).astype(f32)
        return keep + got[:2], (later + got[2:]).astype(bf16)

    bar = lambda *values: lax.optimization_barrier(values)

    (x2, x3), (w0, w1) = (2, 3), (0, 1)
    xa_own, xb_own = slab((x2, x3)), slab((w0, w1))
    wa = jnp.stack([weight, swap(weight, "z", 1)])
    xa = jnp.stack([xa_own, swap(xa_own, "h", 1)])
    wa_near = jnp.stack([wa, swap(wa, "x", ONE_THREE)])
    xa, wa_near, xb_own, quant, order, weight = bar(xa, wa_near, xb_own, quant, order, weight)
    xb = jnp.stack([xb_own, swap(xb_own, "h", 1)])
    wa_far = swap(wa_near, "x", THREE_ONE)
    xa_near = jnp.stack([xa, swap(xa, "y", ONE_THREE)])
    xb, wa_near, wa_far, xa_near, weight = bar(xb, wa_near, wa_far, xa_near, weight)
    w2 = swap(weight, "z", 2)
    xa_far = swap(xa_near, "y", THREE_ONE)
    wa_whole, ia_keep, ia_send = input_grad_terms(
        (w0, w1), wa_near, wa_far, swap(wa_near, "c", 1), swap(wa_far, "c", 1)
    )
    w2, xa_near, xa_far, ia_keep, ia_send, weight = bar(w2, xa_near, xa_far, ia_keep, ia_send, weight)
    w3 = swap(weight, "z", 3)
    ia_keep, ia_send = step1(ia_keep, ia_send, "y")
    xa_whole, ga_keep, ga_later, ga_send = weight_grad_terms((x2, x3), xa_near, xa_far)
    ga_keep, ga_send = core_sum(ga_keep, ga_later, ga_send)
    wb = jnp.stack([w2, w3])
    wb, ia_keep, ia_send, ga_keep, ga_send, xb = bar(wb, ia_keep, ia_send, ga_keep, ga_send, xb)
    xb_near = jnp.stack([xb, swap(xb, "y", ONE_THREE)])
    ia = step2(ia_keep, ia_send, "y")
    ia_send = ia[1].astype(bf16)
    ga_keep, ga_send = step1(ga_keep, ga_send, "x")
    wb_near = jnp.stack([wb, swap(wb, "x", ONE_THREE)])
    xb_near, ia, ia_send, ga_keep, ga_send, wb_near = bar(xb_near, ia, ia_send, ga_keep, ga_send, wb_near)
    ia = (ia[0] + swap(ia_send, "h", 1).astype(f32)).astype(bf16)
    xb_far = swap(xb_near, "y", THREE_ONE)
    wb_far = swap(wb_near, "x", THREE_ONE)
    ia, xb_near, xb_far, wb_near, wb_far, ga_keep, ga_send = bar(
        ia, xb_near, xb_far, wb_near, wb_far, ga_keep, ga_send
    )
    ga = step2(ga_keep, ga_send, "x").astype(bf16)
    wb_near2, wb_far2 = swap(wb_near, "c", 1), swap(wb_far, "c", 1)
    xb_whole, gb_keep, gb_later, gb_send = weight_grad_terms((w0, w1), xb_near, xb_far)
    wb_near, wb_far, wb_near2, wb_far2, gb_send, ga = bar(wb_near, wb_far, wb_near2, wb_far2, gb_send, ga)
    gb_keep, gb_send = core_sum(gb_keep, gb_later, gb_send)
    wb_whole, ib_keep, ib_send = input_grad_terms((x2, x3), wb_near, wb_far, wb_near2, wb_far2)
    gb_keep, gb_send, ib_keep, ib_send, ga = bar(gb_keep, gb_send, ib_keep, ib_send, ga)
    g2 = swap(ga[0], "z", 2)
    ib_keep, ib_send = step1(ib_keep, ib_send, "y")
    gb_keep, gb_send = step1(gb_keep, gb_send, "x")
    g2, ib_keep, ib_send, gb_keep, gb_send, ga = bar(g2, ib_keep, ib_send, gb_keep, gb_send, ga)
    g3 = swap(ga[1], "z", 3)
    ib = step2(ib_keep, ib_send, "y")
    gb = step2(gb_keep, gb_send, "x")
    ib_send, g1 = ib[1].astype(bf16), gb[1].astype(bf16)
    ib, ib_send, gb, g1, g3, xa_whole, xb_whole, wa_whole, wb_whole = bar(
        ib, ib_send, gb, g1, g3, xa_whole, xb_whole, wa_whole, wb_whole
    )
    g1 = swap(g1, "z", 1)
    ib = (ib[0] + swap(ib_send, "h", 1).astype(f32)).astype(bf16)
    (forward_out,) = call(
        forward_kernel,
        "forward",
        (shape((tokens, ff), bf16),),
        (xa_whole, xb_whole, wb_whole, wa_whole),
        FLOPS,
    )
    weight_grad = (gb[0] + g1.astype(f32) + g2.astype(f32) + g3.astype(f32)).astype(bf16)
    parts = [ia[:, :wide], ia[:, wide:], ib[:, :wide], ib[:, wide:]]
    stacked = jnp.stack(parts)
    input_grad = jnp.concatenate(
        [lax.dynamic_index_in_dim(stacked, z ^ k, 0, keepdims=False) for k in range(Z)], axis=1
    )
    return forward_out, input_grad, weight_grad


def solution(mesh):
    fine = Mesh(mesh.devices.reshape(SIZES), AXES)
    fsdp, tp = ("z", "x", "c"), ("h", "y")
    return jax.shard_map(
        per_device,
        mesh=fine,
        in_specs=(P(fsdp + tp, None), P(fsdp, tp), P(fsdp, tp), P(fsdp, None)),
        out_specs=(P(fsdp, tp), P(fsdp + tp, None), P(fsdp, tp)),
        check_vma=False,
    )
```
